512 devices in a mesh: layer: 4 (over y), row: 8 (over z_hi, x), col: 16 (over z_lo, core).
Axes of the slice: x: 4, y: 4, z: 16 (z_hi: 2, z_lo: 8; z = z_hi * 8 + z_lo), core: 2. Of those that a mesh axis runs over, the one named last changes fastest.
Arguments:
- pattern: int32 [1024, 8], replicated, may hold values from 0 to 1023, as said below
- density: float32 [1024, 8, 128, 128], P(('row', 'col'), 'layer'), may hold values from -2.5 to 2.5
Outputs:
- square: float32 [1024, 8, 128, 128], P(('row', 'col'), 'layer')
The draws below stay inside these ranges and needn't reach their ends.
Inputs may be any that keep to these rules, and one draw needn't show every extreme that they name: `pattern`: each block row r lists 8 distinct block columns, all within 8 of r, its own column r among them.
All inputs are finite; a program needn't handle non-finite values.
Results may differ from the reference program's by a relative error of at most 0.0003.
Values sent between devices are 32-bit elements; how exact they have to be, the bound alone decides.
A program may use at most 128 MiB of HBM per device.

```python
import jax
import jax.numpy as jnp
from jax import lax

BS = 128
S = 8
RB = 8
NB = 1024


def draw_pattern(key, part):
    key = jax.random.fold_in(key, 7)
    width_all = 2 * RB + 1
    offsets = jnp.arange(width_all, dtype=jnp.int32) - RB
    rows_all = jnp.arange(NB, dtype=jnp.int32)[:, None]
    candidate = rows_all + offsets[None, :]
    scores = jax.random.randint(key, (NB, width_all), 0, 1 << 18, dtype=jnp.int32) * 256 + jnp.arange(width_all, dtype=jnp.int32)[None, :]
    valid = (candidate >= 0) & (candidate < NB)
    scores = jnp.where(valid, scores, -1)
    scores = jnp.where(offsets[None, :] == 0, 1 << 27, scores)
    values_top, picked = lax.top_k(scores, S)
    return jnp.take_along_axis(candidate, picked, axis=1).astype(jnp.int32)


def levels(key, shape, cuts, smallest, top_value):
    factor_of = 1.0
    for dim, shards_of in cuts:
        draws = jax.random.uniform(jax.random.fold_in(jax.random.fold_in(key, 6), dim), (shards_of,), jnp.float32, smallest / len(cuts), top_value / len(cuts))
        factor_of = factor_of * jnp.repeat(jnp.exp(draws), shape[dim] // shards_of).reshape((-1,) + (1,) * (len(shape) - 1 - dim))
    return factor_of


def scatter_about(own_key, dims, scale, limit, cuts=(), held_as=jnp.bfloat16):
    factor_of = levels(own_key, dims, cuts, -0.22, 0.18) if cuts else 1.0
    entries = jax.random.normal(own_key, dims, jnp.float32) * scale * factor_of
    return jnp.minimum(jnp.maximum(entries, -limit), limit).astype(held_as)


def setup_inputs(seed: int = 0) -> dict:
    key_list = jax.random.split(jax.random.key(seed), 3)
    return {
        "pattern": draw_pattern(jax.random.fold_in(key_list[2], 71), 0),
        "density": scatter_about(key_list[1], (NB, S, BS, BS), ((BS * S) ** -0.25), 2.5, ((0, 128), (1, 4)), jnp.float32),
    }


def reference(pattern, density):
    def one_row(index):
        columns = pattern[index]
        blocks = density[index]
        picked = jnp.take(density, columns, axis=0)
        far_cols = jnp.take(pattern, columns, axis=0)
        match = (far_cols[:, :, None] == columns[None, None, :]).astype(jnp.float32)
        products = jnp.einsum("tij,tujk->tuik", blocks, picked, precision=lax.Precision.HIGHEST)
        return jnp.einsum("tus,tuik->sik", match, products, precision=lax.Precision.HIGHEST)

    return lax.map(one_row, jnp.arange(NB, dtype=jnp.int32))
```

```python
import jax
import jax.numpy as jnp
from jax import lax
from jax.experimental import pallas as pl
from jax.experimental.pallas import tpu as pltpu
from jax.sharding import PartitionSpec as P

MESH = pl.DeviceIdType.MESH
LAYERS, ROWS_AXIS, COLS_AXIS, RUNS = 4, 8, 16, 4
ROWS, SLOTS, QUARTER, BS = 8, 8, 2, 128
BLOCKS = ROWS * QUARTER
GROUP = LAYERS * BLOCKS
CHUNKS = 4
CB = BLOCKS // CHUNKS


def kernel(
    pat_ref, den_ref, out_ref,
    near, part, pat, tab_near, tab_part, a_hi, a_lo, m_hi, m_lo, acc,
    near_sem, part_sem, send_sem, local_sem, pat_sem, out_sem,
):
    l, row, col = (lax.axis_index(a) for a in ("layer", "row", "col"))
    core = lax.rem(col, 2)
    g = row * COLS_AXIS + col
    up, dn, opp = lax.rem(l + 1, 4), lax.rem(l + 3, 4), lax.rem(l + 2, 4)
    pg = lax.rem(g + jnp.where(core == 0, 127, 1), 128)
    at_up, at_dn = (up, row, col), (dn, row, col)
    at_mate = (l, row, col + 1 - 2 * core)
    at_part = (l, lax.div(pg, COLS_AXIS), lax.rem(pg, COLS_AXIS))
    x = lax.rem(row, RUNS)
    far = jnp.logical_or(
        jnp.logical_and(col == 0, x != 0),
        jnp.logical_and(col == COLS_AXIS - 1, x != RUNS - 1),
    )
    close = jnp.logical_not(far)

    barrier = pltpu.get_barrier_semaphore()
    for peer in (at_up, at_dn, at_mate, at_part):
        pl.semaphore_signal(barrier, inc=1, device_id=peer, device_id_type=MESH)

    sent = []

    def send(src, dst, sem, peer, when=None):
        n = len(sent)
        copy = pltpu.make_async_remote_copy(
            src_ref=src, dst_ref=dst, send_sem=send_sem.at[n], recv_sem=sem,
            device_id=peer, device_id_type=MESH,
        )
        sent.append((copy, when))
        if when is None:
            copy.start()
        else:
            pl.when(when)(copy.start)

    def piece(ref, base, layer, j):
        return ref.at[pl.ds(base + layer * BLOCKS + j * CB, CB)]

    def own(layer, j):
        return piece(near, 0, layer, j)

    def mate(layer, j):
        return piece(near, GROUP, layer, j)

    def halo(layer, j):
        return piece(part, 0, layer, j)

    def own_sem(layer, j):
        return near_sem.at[layer * CHUNKS + j]

    def mate_sem(layer, j):
        return near_sem.at[LAYERS * CHUNKS + layer * CHUNKS + j]

    def halo_sem(layer, j):
        return part_sem.at[layer * CHUNKS + j]

    def arrived(ref, sem):
        pltpu.make_async_remote_copy(
            src_ref=ref, dst_ref=ref, send_sem=send_sem.at[0], recv_sem=sem,
            device_id=at_mate, device_id_type=MESH,
        ).wait_recv()

    pat_copies = []
    for k in range(3):
        kg = lax.rem(g + 127 + k, 128)
        c = pltpu.make_async_copy(
            pat_ref.at[pl.ds(pl.multiple_of(kg * ROWS, ROWS), ROWS)], pat.at[pl.ds(k * ROWS, ROWS)], pat_sem.at[k]
        )
        c.start()
        pat_copies.append(c)
    mine = pltpu.make_async_copy(den_ref, near.at[pl.ds(l * BLOCKS, BLOCKS)], local_sem)
    mine.start()
    pl.semaphore_wait(barrier, 4)

    for j in range(CHUNKS):
        src = den_ref.at[pl.ds(j * CB, CB)]
        send(src, halo(l, j), halo_sem(l, j), at_part)
        send(src, own(l, j), own_sem(l, j), at_up)
        send(src, own(l, j), own_sem(l, j), at_dn)
        send(src, mate(l, j), mate_sem(l, j), at_mate)

    near[2 * GROUP] = jnp.zeros((BS, BS), jnp.float32)
    part[GROUP] = jnp.zeros((BS, BS), jnp.float32)
    for c in pat_copies:
        c.wait()

    def index_row(r, carry):
        wanted = [pat[ROWS + r, 2 * l + s] for s in range(QUARTER)]
        for t in range(SLOTS):
            q = jnp.clip(pat[ROWS + r, t] - ROWS * (g - 1), 0, 3 * ROWS - 1)
            grp, qrow = lax.div(q, ROWS), lax.rem(q, ROWS)
            is_own = grp == 1
            is_mate = grp == 2 - 2 * core
            is_near = jnp.logical_or(is_own, is_mate)
            base = qrow * QUARTER
            at = [jnp.int32(-1)] * QUARTER
            for u in range(SLOTS):
                v = pat[q, u]
                for s in range(QUARTER):
                    at[s] = jnp.where(v == wanted[s], base + (u // 2) * BLOCKS + u % 2, at[s])
            for s in range(QUARTER):
                hit = at[s] >= 0
                tab_near[r * 16 + t * 2 + s] = jnp.where(
                    jnp.logical_and(hit, is_near), at[s] + jnp.where(is_own, 0, GROUP), 2 * GROUP
                )
                tab_part[r * 16 + t * 2 + s] = jnp.where(
                    jnp.logical_and(hit, jnp.logical_not(is_near)), at[s], GROUP
                )
        return carry

    lax.fori_loop(0, ROWS, index_row, 0)

    for j in range(CHUNKS):
        arrived(own(dn, j), own_sem(dn, j))
        if j < CHUNKS // 2:
            send(own(dn, j), own(dn, j), own_sem(dn, j), at_up)
        send(own(dn, j), halo(dn, j), halo_sem(dn, j), at_part, close)
        send(own(dn, j), mate(dn, j), mate_sem(dn, j), at_mate)
        arrived(own(up, j), own_sem(up, j))
        if j >= CHUNKS // 2:
            send(own(up, j), own(up, j), own_sem(up, j), at_dn)
        send(own(up, j), halo(up, j), halo_sem(up, j), at_part, close)
        send(own(up, j), mate(up, j), mate_sem(up, j), at_mate)
        arrived(halo(l, j), halo_sem(l, j))
        send(halo(l, j), halo(l, j), halo_sem(l, j), at_up, far)
        send(halo(l, j), halo(l, j), halo_sem(l, j), at_dn, far)
    for j in range(CHUNKS):
        arrived(own(opp, j), own_sem(opp, j))
        send(own(opp, j), mate(opp, j), mate_sem(opp, j), at_mate)
        arrived(halo(dn, j), halo_sem(dn, j))
        if j < CHUNKS // 2:
            send(halo(dn, j), halo(dn, j), halo_sem(dn, j), at_up)
        arrived(halo(up, j), halo_sem(up, j))
        if j >= CHUNKS // 2:
            send(halo(up, j), halo(up, j), halo_sem(up, j), at_dn)
    mine.wait()
    for layer in range(LAYERS):
        for j in range(CHUNKS):
            arrived(mate(layer, j), mate_sem(layer, j))

    def split(v):
        hi = v.astype(jnp.bfloat16)
        return hi, (v - hi.astype(jnp.float32)).astype(jnp.bfloat16)

    def product(r, ref, tab):
        for t in range(SLOTS):
            for s in range(QUARTER):
                hi, lo = split(ref[tab[r * 16 + t * 2 + s]])
                m_hi[t * BS:(t + 1) * BS, s * BS:(s + 1) * BS] = hi
                m_lo[t * BS:(t + 1) * BS, s * BS:(s + 1) * BS] = lo
        h, w = a_hi[r], m_hi[...]
        total = jnp.dot(h, w, preferred_element_type=jnp.float32)
        total += jnp.dot(h, m_lo[...], preferred_element_type=jnp.float32)
        return total + jnp.dot(a_lo[r], w, preferred_element_type=jnp.float32)

    def near_row(r, carry):
        for t in range(SLOTS):
            hi, lo = split(near[(t // 2) * BLOCKS + r * QUARTER + t % 2])
            a_hi[r, :, t * BS:(t + 1) * BS] = hi
            a_lo[r, :, t * BS:(t + 1) * BS] = lo
        total = product(r, near, tab_near)
        for s in range(QUARTER):
            acc[r * QUARTER + s] = total[:, s * BS:(s + 1) * BS]
        return carry

    lax.fori_loop(0, ROWS, near_row, 0)

    for j in range(CHUNKS):
        arrived(halo(opp, j), halo_sem(opp, j))

    def part_row(r, carry):
        total = product(r, part, tab_part)
        for s in range(QUARTER):
            acc[r * QUARTER + s] += total[:, s * BS:(s + 1) * BS]
        return carry

    lax.fori_loop(0, ROWS, part_row, 0)
    done = pltpu.make_async_copy(acc, out_ref, out_sem)
    done.start()
    for copy, when in sent:
        if when is None:
            copy.wait_send()
        else:
            pl.when(when)(copy.wait_send)
    done.wait()


def per_device(pattern, density):
    shape = density.shape
    flat = density.reshape(BLOCKS, BS, BS)
    f32, bf16 = jnp.float32, jnp.bfloat16
    result = pl.pallas_call(
        kernel,
        out_shape=jax.ShapeDtypeStruct((BLOCKS, BS, BS), f32),
        in_specs=[pl.BlockSpec(memory_space=pl.ANY)] * 2,
        out_specs=pl.BlockSpec(memory_space=pl.ANY),
        scratch_shapes=[
            pltpu.VMEM((2 * GROUP + 1, BS, BS), f32),
            pltpu.VMEM((GROUP + 1, BS, BS), f32),
            pltpu.SMEM((3 * ROWS, SLOTS), jnp.int32),
            pltpu.SMEM((ROWS * SLOTS * QUARTER,), jnp.int32),
            pltpu.SMEM((ROWS * SLOTS * QUARTER,), jnp.int32),
            pltpu.VMEM((ROWS, BS, SLOTS * BS), bf16),
            pltpu.VMEM((ROWS, BS, SLOTS * BS), bf16),
            pltpu.VMEM((SLOTS * BS, QUARTER * BS), bf16),
            pltpu.VMEM((SLOTS * BS, QUARTER * BS), bf16),
            pltpu.VMEM((BLOCKS, BS, BS), f32),
            pltpu.SemaphoreType.DMA((2 * LAYERS * CHUNKS,)),
            pltpu.SemaphoreType.DMA((LAYERS * CHUNKS,)),
            pltpu.SemaphoreType.DMA((13 * CHUNKS,)),
            pltpu.SemaphoreType.DMA,
            pltpu.SemaphoreType.DMA((3,)),
            pltpu.SemaphoreType.DMA,
        ],
        compiler_params=pltpu.CompilerParams(
            collective_id=0, has_side_effects=True, vmem_limit_bytes=40 * 1024 * 1024
        ),
        cost_estimate=pl.CostEstimate(flops=3 * 2**29, bytes_accessed=2**24, transcendentals=0),
    )(pattern, flat)
    return result.reshape(shape)


def solution(mesh):
    in_specs = (P(), P(("row", "col"), "layer", None, None))
    out_specs = P(("row", "col"), "layer", None, None)
    return jax.shard_map(
        per_device, mesh=mesh, in_specs=in_specs, out_specs=out_specs, check_vma=False
    )
```

```python
import jax
import jax.numpy as jnp
from jax import lax
from jax.experimental import pallas as pl
from jax.experimental.pallas import tpu as pltpu
from jax.sharding import PartitionSpec as P

MESH = pl.DeviceIdType.MESH
LAYERS, ROWS_AXIS, COLS_AXIS, RUNS = 4, 8, 16, 4
ROWS, SLOTS, QUARTER, BS = 8, 8, 2, 128
BLOCKS = ROWS * QUARTER
GROUP = LAYERS * BLOCKS
TILE = COLS_AXIS * ROWS
REACH = SLOTS - 1
CHUNKS = 4
AHEAD = 4
DIRECT = (1, 2)
CB = BLOCKS // CHUNKS


def kernel(
    pat_ref, den_ref, out_ref,
    near, part, pat, tab_near, tab_part, tab_t, a_hi, a_lo, m_hi, m_lo, acc,
    near_sem, part_sem, send_sem, local_sem, pat_sem,
):
    l, row, col = (lax.axis_index(a) for a in ("layer", "row", "col"))
    core = lax.rem(col, 2)
    g = row * COLS_AXIS + col
    up, dn, opp = lax.rem(l + 1, 4), lax.rem(l + 3, 4), lax.rem(l + 2, 4)
    pg = lax.rem(g + jnp.where(core == 0, 127, 1), 128)
    at_up, at_dn = (up, row, col), (dn, row, col)
    at_mate = (l, row, col + 1 - 2 * core)
    at_part = (l, lax.div(pg, COLS_AXIS), lax.rem(pg, COLS_AXIS))

    def long_way(at_row, at_col):
        at_x = lax.rem(at_row, RUNS)
        return jnp.logical_or(
            jnp.logical_and(at_col == 0, at_x != 0),
            jnp.logical_and(at_col == COLS_AXIS - 1, at_x != RUNS - 1),
        )

    def mate_col(at_col):
        return at_col + 1 - 2 * lax.rem(at_col, 2)

    far = long_way(row, col)
    close = jnp.logical_not(far)
    keep = jnp.logical_not(long_way(row, mate_col(col)))
    give = long_way(at_part[1], mate_col(at_part[2]))

    barrier = pltpu.get_barrier_semaphore()
    for peer in (at_up, at_dn, at_mate, at_part):
        pl.semaphore_signal(barrier, inc=1, device_id=peer, device_id_type=MESH)

    sent = []

    def send(src, dst, sem, peer, when=None):
        n = len(sent)
        copy = pltpu.make_async_remote_copy(
            src_ref=src, dst_ref=dst, send_sem=send_sem.at[n], recv_sem=sem,
            device_id=peer, device_id_type=MESH,
        )
        sent.append((copy, when))
        if when is None:
            copy.start()
        else:
            pl.when(when)(copy.start)

    def piece(ref, base, layer, j):
        return ref.at[pl.ds(base + layer * BLOCKS + j * CB, CB)]

    def own(layer, j):
        return piece(near, 0, layer, j)

    def mate(layer, j):
        return piece(near, GROUP, layer, j)

    def halo(layer, j):
        return piece(part, 0, layer, j)

    def own_sem(layer, j):
        return near_sem.at[layer * CHUNKS + j]

    def mate_sem(layer, j):
        return near_sem.at[LAYERS * CHUNKS + layer * CHUNKS + j]

    def halo_sem(layer, j):
        return part_sem.at[layer * CHUNKS + j]

    def arrived(ref, sem):
        pltpu.make_async_remote_copy(
            src_ref=ref, dst_ref=ref, send_sem=send_sem.at[0], recv_sem=sem,
            device_id=at_mate, device_id_type=MESH,
        ).wait_recv()

    pat_copies = []
    for k in range(3):
        tile = lax.rem(row + ROWS_AXIS - 1 + k, ROWS_AXIS)
        c = pltpu.make_async_copy(
            pat_ref.at[:, pl.ds(pl.multiple_of(tile * TILE, TILE), TILE)], pat.at[pl.ds(k * SLOTS, SLOTS)], pat_sem.at[k]
        )
        c.start()
        pat_copies.append(c)
    mine = pltpu.make_async_copy(den_ref, near.at[pl.ds(l * BLOCKS, BLOCKS)], local_sem)
    mine.start()
    pl.semaphore_wait(barrier, 4)

    def spread(j):
        src = den_ref.at[pl.ds(j * CB, CB)]
        send(src, own(l, j), own_sem(l, j), at_up)
        send(src, own(l, j), own_sem(l, j), at_dn)

    for j in range(CHUNKS):
        src = den_ref.at[pl.ds(j * CB, CB)]
        if j < AHEAD:
            spread(j)
        send(src, halo(l, j), halo_sem(l, j), at_part)
    for j in range(CHUNKS):
        src = den_ref.at[pl.ds(j * CB, CB)]
        send(src, mate(l, j), mate_sem(l, j), at_mate)

    near[2 * GROUP] = jnp.zeros((BS, BS), jnp.float32)
    part[GROUP] = jnp.zeros((BS, BS), jnp.float32)
    for c in pat_copies:
        c.wait()

    def index_row(r, carry):
        here = col * ROWS + r
        wanted = [pat[SLOTS + 2 * l + s, here] for s in range(QUARTER)]
        count = jnp.int32(0)
        far_t = [jnp.int32(0)] * SLOTS
        far_at = [[jnp.int32(GROUP)] * QUARTER for _ in range(SLOTS)]
        for t in range(SLOTS):
            q = jnp.clip(pat[SLOTS + t, here] - TILE * (row - 1), 0, 3 * TILE - 1)
            side, lane = lax.div(q, TILE) * SLOTS, lax.rem(q, TILE)
            grp, qrow = lax.div(q, ROWS) - COLS_AXIS - col, lax.rem(q, ROWS)
            is_own = grp == 0
            is_near = jnp.logical_or(is_own, grp == 1 - 2 * core)
            base = qrow * QUARTER
            at = [jnp.int32(-1)] * QUARTER
            for u in range(SLOTS):
                v = pat[side + u, lane]
                for s in range(QUARTER):
                    at[s] = jnp.where(v == wanted[s], base + (u // 2) * BLOCKS + u % 2, at[s])
            for s in range(QUARTER):
                hit = jnp.logical_and(at[s] >= 0, is_near)
                tab_near[r * 16 + t * 2 + s] = jnp.where(
                    hit, at[s] + jnp.where(is_own, 0, GROUP), 2 * GROUP
                )
            is_far = jnp.logical_not(is_near)
            for j in range(min(t + 1, REACH)):
                here_j = jnp.logical_and(is_far, count == j)
                far_t[j] = jnp.where(here_j, t, far_t[j])
                for s in range(QUARTER):
                    far_at[j][s] = jnp.where(jnp.logical_and(here_j, at[s] >= 0), at[s], far_at[j][s])
            count = count + is_far.astype(jnp.int32)
        for j in range(SLOTS):
            tab_t[r * SLOTS + j] = far_t[j]
            for s in range(QUARTER):
                tab_part[r * 16 + j * 2 + s] = far_at[j][s]
        return carry

    lax.fori_loop(0, ROWS, index_row, 0)

    half = CHUNKS // 2
    for j in range(CHUNKS):
        arrived(own(dn, j), own_sem(dn, j))
        arrived(own(up, j), own_sem(up, j))
        if j + AHEAD < CHUNKS:
            spread(j + AHEAD)
        if j < half:
            send(own(dn, j), own(dn, j), own_sem(dn, j), at_up)
        else:
            send(own(up, j), own(up, j), own_sem(up, j), at_dn)
        if j < half:
            send(own(dn, j), halo(dn, j), halo_sem(dn, j), at_part, close)
        else:
            send(own(up, j), halo(up, j), halo_sem(up, j), at_part, close)
        send(own(dn, j), mate(dn, j), mate_sem(dn, j), at_mate)
        send(own(up, j), mate(up, j), mate_sem(up, j), at_mate)
    for j in range(half):
        send(own(dn, j + half), halo(dn, j + half), halo_sem(dn, j + half), at_part, close)
        send(own(up, j), halo(up, j), halo_sem(up, j), at_part, close)
    for j in range(CHUNKS):
        arrived(halo(l, j), halo_sem(l, j))
        send(halo(l, j), halo(l, j), halo_sem(l, j), at_up, far)
        send(halo(l, j), halo(l, j), halo_sem(l, j), at_dn, far)
    for j in range(half):
        for k in (j, j + half):
            arrived(own(opp, k), own_sem(opp, k))
            send(own(opp, k), mate(opp, k), mate_sem(opp, k), at_mate)
            if k in DIRECT:
                send(own(opp, k), halo(opp, k), halo_sem(opp, k), at_part, give)
    for j in range(half):
        arrived(halo(dn, j), halo_sem(dn, j))
        send(halo(dn, j), halo(dn, j), halo_sem(dn, j), at_up, keep if j in DIRECT else None)
        arrived(halo(up, j + half), halo_sem(up, j + half))
        send(halo(up, j + half), halo(up, j + half), halo_sem(up, j + half), at_dn, keep if j + half in DIRECT else None)
    for j in range(half):
        arrived(halo(dn, j + half), halo_sem(dn, j + half))
        arrived(halo(up, j), halo_sem(up, j))
    mine.wait()
    for layer in range(LAYERS):
        for j in range(CHUNKS):
            arrived(mate(layer, j), mate_sem(layer, j))

    def split(v):
        hi = v.astype(jnp.bfloat16)
        return hi, (v - hi.astype(jnp.float32)).astype(jnp.bfloat16)

    def product(r, ref, tab):
        for t in range(SLOTS):
            for s in range(QUARTER):
                hi, lo = split(ref[tab[r * 16 + t * 2 + s]])
                m_hi[t * BS:(t + 1) * BS, s * BS:(s + 1) * BS] = hi
                m_lo[t * BS:(t + 1) * BS, s * BS:(s + 1) * BS] = lo
        h, low = (jnp.concatenate([a[r * SLOTS + t] for t in range(SLOTS)], axis=1) for a in (a_hi, a_lo))
        w = m_hi[...]
        total = jnp.dot(h, w, preferred_element_type=jnp.float32)
        total += jnp.dot(h, m_lo[...], preferred_element_type=jnp.float32)
        return total + jnp.dot(low, w, preferred_element_type=jnp.float32)

    def near_row(r, carry):
        for t in range(SLOTS):
            hi, lo = split(near[(t // 2) * BLOCKS + r * QUARTER + t % 2])
            a_hi[r * SLOTS + t] = hi
            a_lo[r * SLOTS + t] = lo
        total = product(r, near, tab_near)
        for s in range(QUARTER):
            acc[r * QUARTER + s] = total[:, s * BS:(s + 1) * BS]
        return carry

    lax.fori_loop(0, ROWS, near_row, 0)

    for j in range(CHUNKS):
        arrived(halo(opp, j), halo_sem(opp, j))

    def pair(r, j):
        tiles = [[split(part[tab_part[r * 16 + i * 2 + s]]) for s in range(QUARTER)] for i in (j, j + 1)]
        w_hi, w_lo = (
            jnp.concatenate([jnp.concatenate([b[k] for b in tile], axis=1) for tile in tiles], axis=0) for k in (0, 1)
        )
        h, low = (jnp.concatenate([a[r * SLOTS + tab_t[r * SLOTS + i]] for i in (j, j + 1)], axis=1) for a in (a_hi, a_lo))
        total = jnp.dot(h, w_hi, preferred_element_type=jnp.float32)
        total += jnp.dot(h, w_lo, preferred_element_type=jnp.float32)
        return total + jnp.dot(low, w_hi, preferred_element_type=jnp.float32)

    for i in range(ROWS):
        r = i + core * (ROWS - 1 - 2 * i)
        total = pair(r, 0)
        for j in range(2, min(REACH, ROWS - i), 2):
            total += pair(r, j)
        for s in range(QUARTER):
            out_ref[r * QUARTER + s] = acc[r * QUARTER + s] + total[:, s * BS:(s + 1) * BS]
    for copy, when in sent:
        if when is None:
            copy.wait_send()
        else:
            pl.when(when)(copy.wait_send)


def per_device(pattern, density):
    shape = density.shape
    flat = density.reshape(BLOCKS, BS, BS)
    f32, bf16 = jnp.float32, jnp.bfloat16
    result = pl.pallas_call(
        kernel,
        out_shape=jax.ShapeDtypeStruct((BLOCKS, BS, BS), f32),
        in_specs=[pl.BlockSpec(memory_space=pl.ANY)] * 2,
        out_specs=pl.BlockSpec(memory_space=pltpu.VMEM),
        scratch_shapes=[
            pltpu.VMEM((2 * GROUP + 1, BS, BS), f32),
            pltpu.VMEM((GROUP + 1, BS, BS), f32),
            pltpu.SMEM((3 * SLOTS, TILE), jnp.int32),
            pltpu.SMEM((ROWS * SLOTS * QUARTER,), jnp.int32),
            pltpu.SMEM((ROWS * SLOTS * QUARTER,), jnp.int32),
            pltpu.SMEM((ROWS * SLOTS,), jnp.int32),
            pltpu.VMEM((ROWS * SLOTS, BS, BS), bf16),
            pltpu.VMEM((ROWS * SLOTS, BS, BS), bf16),
            pltpu.VMEM((SLOTS * BS, QUARTER * BS), bf16),
            pltpu.VMEM((SLOTS * BS, QUARTER * BS), bf16),
            pltpu.VMEM((BLOCKS, BS, BS), f32),
            pltpu.SemaphoreType.DMA((2 * LAYERS * CHUNKS,)),
            pltpu.SemaphoreType.DMA((LAYERS * CHUNKS,)),
            pltpu.SemaphoreType.DMA((13 * CHUNKS + len(DIRECT),)),
            pltpu.SemaphoreType.DMA,
            pltpu.SemaphoreType.DMA((3,)),
        ],
        compiler_params=pltpu.CompilerParams(
            collective_id=0, has_side_effects=True, vmem_limit_bytes=40 * 1024 * 1024
        ),
        cost_estimate=pl.CostEstimate(flops=3 * 2**29, bytes_accessed=2**24, transcendentals=0),
    )(pattern.T, flat)
    return result.reshape(shape)


def solution(mesh):
    in_specs = (P(), P(("row", "col"), "layer", None, None))
    out_specs = P(("row", "col"), "layer", None, None)
    return jax.shard_map(
        per_device, mesh=mesh, in_specs=in_specs, out_specs=out_specs, check_vma=False
    )
```

```python
import jax
import jax.numpy as jnp
from jax import lax
from jax.experimental import pallas as pl
from jax.experimental.pallas import tpu as pltpu
from jax.sharding import PartitionSpec as P

MESH = pl.DeviceIdType.MESH
LAYERS, ROWS_AXIS, COLS_AXIS, RUNS = 4, 8, 16, 4
ROWS, SLOTS, QUARTER, BS = 8, 8, 2, 128
BLOCKS = ROWS * QUARTER
GROUP = LAYERS * BLOCKS
TILE = COLS_AXIS * ROWS
REACH = SLOTS - 1
CHUNKS = 4
AHEAD = 4
DIRECT = (0, 2)
CB = BLOCKS // CHUNKS


def kernel(
    pat_ref, den_ref, out_ref,
    near, part, pat, tab_near, tab_part, tab_t, a_hi, a_lo, m_hi, m_lo, acc,
    near_sem, part_sem, send_sem, local_sem, pat_sem,
):
    l, row, col = (lax.axis_index(a) for a in ("layer", "row", "col"))
    core = lax.rem(col, 2)
    g = row * COLS_AXIS + col
    up, dn, opp = lax.rem(l + 1, 4), lax.rem(l + 3, 4), lax.rem(l + 2, 4)
    pg = lax.rem(g + jnp.where(core == 0, 127, 1), 128)
    at_up, at_dn = (up, row, col), (dn, row, col)
    at_mate = (l, row, col + 1 - 2 * core)
    at_part = (l, lax.div(pg, COLS_AXIS), lax.rem(pg, COLS_AXIS))

    def long_way(at_row, at_col):
        at_x = lax.rem(at_row, RUNS)
        return jnp.logical_or(
            jnp.logical_and(at_col == 0, at_x != 0),
            jnp.logical_and(at_col == COLS_AXIS - 1, at_x != RUNS - 1),
        )

    def mate_col(at_col):
        return at_col + 1 - 2 * lax.rem(at_col, 2)

    far = long_way(row, col)
    close = jnp.logical_not(far)
    keep = jnp.logical_not(long_way(row, mate_col(col)))
    give = long_way(at_part[1], mate_col(at_part[2]))

    barrier = pltpu.get_barrier_semaphore()
    for peer in (at_up, at_dn, at_mate, at_part):
        pl.semaphore_signal(barrier, inc=1, device_id=peer, device_id_type=MESH)

    sent = []

    def send(src, dst, sem, peer, when=None):
        n = len(sent)
        copy = pltpu.make_async_remote_copy(
            src_ref=src, dst_ref=dst, send_sem=send_sem.at[n], recv_sem=sem,
            device_id=peer, device_id_type=MESH,
        )
        sent.append((copy, when))
        if when is None:
            copy.start()
        else:
            pl.when(when)(copy.start)

    def piece(ref, base, layer, j):
        return ref.at[pl.ds(base + layer * BLOCKS + j * CB, CB)]

    def own(layer, j):
        return piece(near, 0, layer, j)

    def mate(layer, j):
        return piece(near, GROUP, layer, j)

    def halo(layer, j):
        return piece(part, 0, layer, j)

    def own_sem(layer, j):
        return near_sem.at[layer * CHUNKS + j]

    def mate_sem(layer, j):
        return near_sem.at[LAYERS * CHUNKS + layer * CHUNKS + j]

    def halo_sem(layer, j):
        return part_sem.at[layer * CHUNKS + j]

    def arrived(ref, sem):
        pltpu.make_async_remote_copy(
            src_ref=ref, dst_ref=ref, send_sem=send_sem.at[0], recv_sem=sem,
            device_id=at_mate, device_id_type=MESH,
        ).wait_recv()

    pat_copies = []
    for k in range(3):
        tile = lax.rem(row + ROWS_AXIS - 1 + k, ROWS_AXIS)
        c = pltpu.make_async_copy(
            pat_ref.at[:, pl.ds(pl.multiple_of(tile * TILE, TILE), TILE)], pat.at[pl.ds(k * SLOTS, SLOTS)], pat_sem.at[k]
        )
        c.start()
        pat_copies.append(c)
    mine = pltpu.make_async_copy(den_ref, near.at[pl.ds(l * BLOCKS, BLOCKS)], local_sem)
    mine.start()
    pl.semaphore_wait(barrier, 4)

    def spread(j):
        src = den_ref.at[pl.ds(j * CB, CB)]
        send(src, own(l, j), own_sem(l, j), at_up)
        send(src, own(l, j), own_sem(l, j), at_dn)

    for j in range(CHUNKS):
        src = den_ref.at[pl.ds(j * CB, CB)]
        if j < AHEAD:
            spread(j)
        send(src, halo(l, j), halo_sem(l, j), at_part)
    for j in range(CHUNKS):
        src = den_ref.at[pl.ds(j * CB, CB)]
        send(src, mate(l, j), mate_sem(l, j), at_mate)

    near[2 * GROUP] = jnp.zeros((BS, BS), jnp.float32)
    part[GROUP] = jnp.zeros((BS, BS), jnp.float32)
    for c in pat_copies:
        c.wait()

    def index_row(r, carry):
        here = col * ROWS + r
        wanted = [pat[SLOTS + 2 * l + s, here] for s in range(QUARTER)]
        count = jnp.int32(0)
        far_t = [jnp.int32(0)] * SLOTS
        far_at = [[jnp.int32(GROUP)] * QUARTER for _ in range(SLOTS)]
        for t in range(SLOTS):
            q = jnp.clip(pat[SLOTS + t, here] - TILE * (row - 1), 0, 3 * TILE - 1)
            side, lane = lax.div(q, TILE) * SLOTS, lax.rem(q, TILE)
            grp, qrow = lax.div(q, ROWS) - COLS_AXIS - col, lax.rem(q, ROWS)
            is_own = grp == 0
            is_near = jnp.logical_or(is_own, grp == 1 - 2 * core)
            base = qrow * QUARTER
            at = [jnp.int32(-1)] * QUARTER
            for u in range(SLOTS):
                v = pat[side + u, lane]
                for s in range(QUARTER):
                    at[s] = jnp.where(v == wanted[s], base + (u // 2) * BLOCKS + u % 2, at[s])
            for s in range(QUARTER):
                hit = jnp.logical_and(at[s] >= 0, is_near)
                tab_near[r * 16 + t * 2 + s] = jnp.where(
                    hit, at[s] + jnp.where(is_own, 0, GROUP), 2 * GROUP
                )
            is_far = jnp.logical_not(is_near)
            for j in range(min(t + 1, REACH)):
                here_j = jnp.logical_and(is_far, count == j)
                far_t[j] = jnp.where(here_j, t, far_t[j])
                for s in range(QUARTER):
                    far_at[j][s] = jnp.where(jnp.logical_and(here_j, at[s] >= 0), at[s], far_at[j][s])
            count = count + is_far.astype(jnp.int32)
        for j in range(SLOTS):
            tab_t[r * SLOTS + j] = far_t[j]
            for s in range(QUARTER):
                tab_part[r * 16 + j * 2 + s] = far_at[j][s]
        return carry

    lax.fori_loop(0, ROWS, index_row, 0)

    half = CHUNKS // 2
    for j in range(CHUNKS):
        arrived(own(dn, j), own_sem(dn, j))
        arrived(own(up, j), own_sem(up, j))
        if j + AHEAD < CHUNKS:
            spread(j + AHEAD)
        if j < half:
            send(own(dn, j), own(dn, j), own_sem(dn, j), at_up)
        else:
            send(own(up, j), own(up, j), own_sem(up, j), at_dn)
        if j < half:
            send(own(dn, j), halo(dn, j), halo_sem(dn, j), at_part, close)
        else:
            send(own(up, j), halo(up, j), halo_sem(up, j), at_part, close)
        send(own(dn, j), mate(dn, j), mate_sem(dn, j), at_mate)
        send(own(up, j), mate(up, j), mate_sem(up, j), at_mate)
    for j in range(half):
        send(own(dn, j + half), halo(dn, j + half), halo_sem(dn, j + half), at_part, close)
        send(own(up, j), halo(up, j), halo_sem(up, j), at_part, close)
    for j in range(CHUNKS):
        arrived(halo(l, j), halo_sem(l, j))
        send(halo(l, j), halo(l, j), halo_sem(l, j), at_up, far)
        send(halo(l, j), halo(l, j), halo_sem(l, j), at_dn, far)
    for j in range(half):
        for k in (j, j + half):
            arrived(own(opp, k), own_sem(opp, k))
            send(own(opp, k), mate(opp, k), mate_sem(opp, k), at_mate)
            if k in DIRECT:
                send(own(opp, k), halo(opp, k), halo_sem(opp, k), at_part, give)
    for j in range(half):
        arrived(halo(dn, j), halo_sem(dn, j))
        send(halo(dn, j), halo(dn, j), halo_sem(dn, j), at_up, keep if j in DIRECT else None)
        arrived(halo(up, j + half), halo_sem(up, j + half))
        send(halo(up, j + half), halo(up, j + half), halo_sem(up, j + half), at_dn, keep if j + half in DIRECT else None)
    for j in range(half):
        arrived(halo(dn, j + half), halo_sem(dn, j + half))
        arrived(halo(up, j), halo_sem(up, j))
    mine.wait()
    for layer in range(LAYERS):
        for j in range(CHUNKS):
            arrived(mate(layer, j), mate_sem(layer, j))

    def split(v):
        hi = v.astype(jnp.bfloat16)
        return hi, (v - hi.astype(jnp.float32)).astype(jnp.bfloat16)

    def product(r, ref, tab):
        for t in range(SLOTS):
            for s in range(QUARTER):
                hi, lo = split(ref[tab[r * 16 + t * 2 + s]])
                m_hi[t * BS:(t + 1) * BS, s * BS:(s + 1) * BS] = hi
                m_lo[t * BS:(t + 1) * BS, s * BS:(s + 1) * BS] = lo
        h, low = (jnp.concatenate([a[r * SLOTS + t] for t in range(SLOTS)], axis=1) for a in (a_hi, a_lo))
        w = m_hi[...]
        total = jnp.dot(h, w, preferred_element_type=jnp.float32)
        total += jnp.dot(h, m_lo[...], preferred_element_type=jnp.float32)
        return total + jnp.dot(low, w, preferred_element_type=jnp.float32)

    def near_row(r, carry):
        for t in range(SLOTS):
            hi, lo = split(near[(t // 2) * BLOCKS + r * QUARTER + t % 2])
            a_hi[r * SLOTS + t] = hi
            a_lo[r * SLOTS + t] = lo
        total = product(r, near, tab_near)
        for s in range(QUARTER):
            acc[r * QUARTER + s] = total[:, s * BS:(s + 1) * BS]
        return carry

    lax.fori_loop(0, ROWS, near_row, 0)

    for j in range(CHUNKS):
        arrived(halo(opp, j), halo_sem(opp, j))

    def pair(r, j):
        tiles = [[split(part[tab_part[r * 16 + i * 2 + s]]) for s in range(QUARTER)] for i in (j, j + 1)]
        w_hi, w_lo = (
            jnp.concatenate([jnp.concatenate([b[k] for b in tile], axis=1) for tile in tiles], axis=0) for k in (0, 1)
        )
        h, low = (jnp.concatenate([a[r * SLOTS + tab_t[r * SLOTS + i]] for i in (j, j + 1)], axis=1) for a in (a_hi, a_lo))
        total = jnp.dot(h, w_hi, preferred_element_type=jnp.float32)
        total += jnp.dot(h, w_lo, preferred_element_type=jnp.float32)
        return total + jnp.dot(low, w_hi, preferred_element_type=jnp.float32)

    for i in range(ROWS):
        r = i + core * (ROWS - 1 - 2 * i)
        total = pair(r, 0)
        for j in range(2, min(REACH, ROWS - i), 2):
            total += pair(r, j)
        for s in range(QUARTER):
            out_ref[r * QUARTER + s] = acc[r * QUARTER + s] + total[:, s * BS:(s + 1) * BS]
    for copy, when in sent:
        if when is None:
            copy.wait_send()
        else:
            pl.when(when)(copy.wait_send)


def per_device(pattern, density):
    shape = density.shape
    flat = density.reshape(BLOCKS, BS, BS)
    f32, bf16 = jnp.float32, jnp.bfloat16
    result = pl.pallas_call(
        kernel,
        out_shape=jax.ShapeDtypeStruct((BLOCKS, BS, BS), f32),
        in_specs=[pl.BlockSpec(memory_space=pl.ANY)] * 2,
        out_specs=pl.BlockSpec(memory_space=pltpu.VMEM),
        scratch_shapes=[
            pltpu.VMEM((2 * GROUP + 1, BS, BS), f32),
            pltpu.VMEM((GROUP + 1, BS, BS), f32),
            pltpu.SMEM((3 * SLOTS, TILE), jnp.int32),
            pltpu.SMEM((ROWS * SLOTS * QUARTER,), jnp.int32),
            pltpu.SMEM((ROWS * SLOTS * QUARTER,), jnp.int32),
            pltpu.SMEM((ROWS * SLOTS,), jnp.int32),
            pltpu.VMEM((ROWS * SLOTS, BS, BS), bf16),
            pltpu.VMEM((ROWS * SLOTS, BS, BS), bf16),
            pltpu.VMEM((SLOTS * BS, QUARTER * BS), bf16),
            pltpu.VMEM((SLOTS * BS, QUARTER * BS), bf16),
            pltpu.VMEM((BLOCKS, BS, BS), f32),
            pltpu.SemaphoreType.DMA((2 * LAYERS * CHUNKS,)),
            pltpu.SemaphoreType.DMA((LAYERS * CHUNKS,)),
            pltpu.SemaphoreType.DMA((13 * CHUNKS + len(DIRECT),)),
            pltpu.SemaphoreType.DMA,
            pltpu.SemaphoreType.DMA((3,)),
        ],
        compiler_params=pltpu.CompilerParams(
            collective_id=0, has_side_effects=True, vmem_limit_bytes=52 * 1024 * 1024
        ),
        cost_estimate=pl.CostEstimate(flops=3 * 2**29, bytes_accessed=2**24, transcendentals=0),
    )(pattern.T, flat)
    return result.reshape(shape)


def solution(mesh):
    in_specs = (P(), P(("row", "col"), "layer", None, None))
    out_specs = P(("row", "col"), "layer", None, None)
    return jax.shard_map(
        per_device, mesh=mesh, in_specs=in_specs, out_specs=out_specs, check_vma=False
    )
```

```python
import jax
import jax.numpy as jnp
from jax import lax
from jax.experimental import pallas as pl
from jax.experimental.pallas import tpu as pltpu
from jax.sharding import PartitionSpec as P

MESH = pl.DeviceIdType.MESH
LAYERS, ROWS_AXIS, COLS_AXIS, RUNS = 4, 8, 16, 4
ROWS, SLOTS, QUARTER, BS = 8, 8, 2, 128
BLOCKS = ROWS * QUARTER
GROUP = LAYERS * BLOCKS
TILE = COLS_AXIS * ROWS
REACH = SLOTS - 1
CHUNKS = 4
DIRECT = (0, 2)
CB = BLOCKS // CHUNKS


def kernel(
    pat_ref, den_ref, out_ref,
    near, part, pat, tab_near, tab_part, tab_t, a_hi, a_lo, m_hi, m_lo, acc,
    near_sem, part_sem, send_sem, local_sem, pat_sem,
):
    l, row, col = (lax.axis_index(a) for a in ("layer", "row", "col"))
    core = lax.rem(col, 2)
    g = row * COLS_AXIS + col
    up, dn, opp = lax.rem(l + 1, 4), lax.rem(l + 3, 4), lax.rem(l + 2, 4)
    pg = lax.rem(g + jnp.where(core == 0, 127, 1), 128)
    at_up, at_dn = (up, row, col), (dn, row, col)
    at_mate = (l, row, col + 1 - 2 * core)
    at_part = (l, lax.div(pg, COLS_AXIS), lax.rem(pg, COLS_AXIS))

    def long_way(at_row, at_col):
        at_x = lax.rem(at_row, RUNS)
        return jnp.logical_or(
            jnp.logical_and(at_col == 0, at_x != 0),
            jnp.logical_and(at_col == COLS_AXIS - 1, at_x != RUNS - 1),
        )

    def mate_col(at_col):
        return at_col + 1 - 2 * lax.rem(at_col, 2)

    far = long_way(row, col)
    close = jnp.logical_not(far)
    keep = jnp.logical_not(long_way(row, mate_col(col)))
    give = long_way(at_part[1], mate_col(at_part[2]))

    barrier = pltpu.get_barrier_semaphore()
    for peer in (at_up, at_dn, at_mate, at_part):
        pl.semaphore_signal(barrier, inc=1, device_id=peer, device_id_type=MESH)

    sent = []

    def send(src, dst, sem, peer, when=None):
        n = len(sent)
        copy = pltpu.make_async_remote_copy(
            src_ref=src, dst_ref=dst, send_sem=send_sem.at[n], recv_sem=sem,
            device_id=peer, device_id_type=MESH,
        )
        sent.append((copy, when))
        if when is None:
            copy.start()
        else:
            pl.when(when)(copy.start)

    def piece(ref, base, layer, j):
        return ref.at[pl.ds(base + layer * BLOCKS + j * CB, CB)]

    def own(layer, j):
        return piece(near, 0, layer, j)

    def mate(layer, j):
        return piece(near, GROUP, layer, j)

    def halo(layer, j):
        return piece(part, 0, layer, j)

    def own_sem(layer, j):
        return near_sem.at[layer * CHUNKS + j]

    def mate_sem(layer, j):
        return near_sem.at[LAYERS * CHUNKS + layer * CHUNKS + j]

    def halo_sem(layer, j):
        return part_sem.at[layer * CHUNKS + j]

    def arrived(ref, sem):
        pltpu.make_async_remote_copy(
            src_ref=ref, dst_ref=ref, send_sem=send_sem.at[0], recv_sem=sem,
            device_id=at_mate, device_id_type=MESH,
        ).wait_recv()

    pat_copies = []
    for k in range(3):
        tile = lax.rem(row + ROWS_AXIS - 1 + k, ROWS_AXIS)
        c = pltpu.make_async_copy(
            pat_ref.at[:, pl.ds(pl.multiple_of(tile * TILE, TILE), TILE)], pat.at[pl.ds(k * SLOTS, SLOTS)], pat_sem.at[k]
        )
        c.start()
        pat_copies.append(c)
    mine = pltpu.make_async_copy(den_ref, near.at[pl.ds(l * BLOCKS, BLOCKS)], local_sem)
    mine.start()
    pl.semaphore_wait(barrier, 4)

    half = CHUNKS // 2

    def later(j):
        return (j + half) % CHUNKS

    for j in range(CHUNKS):
        src = den_ref.at[pl.ds(j * CB, CB)]
        other = den_ref.at[pl.ds(later(j) * CB, CB)]
        send(src, halo(l, j), halo_sem(l, j), at_part)
        send(src, own(l, j), own_sem(l, j), at_up)
        send(other, own(l, later(j)), own_sem(l, later(j)), at_dn)
    for j in range(CHUNKS):
        src = den_ref.at[pl.ds(j * CB, CB)]
        send(src, mate(l, j), mate_sem(l, j), at_mate)

    near[2 * GROUP] = jnp.zeros((BS, BS), jnp.float32)
    part[GROUP] = jnp.zeros((BS, BS), jnp.float32)
    for c in pat_copies:
        c.wait()

    def index_row(r, carry):
        here = col * ROWS + r
        wanted = [pat[SLOTS + 2 * l + s, here] for s in range(QUARTER)]
        count = jnp.int32(0)
        far_t = [jnp.int32(0)] * SLOTS
        far_at = [[jnp.int32(GROUP)] * QUARTER for _ in range(SLOTS)]
        for t in range(SLOTS):
            q = jnp.clip(pat[SLOTS + t, here] - TILE * (row - 1), 0, 3 * TILE - 1)
            side, lane = lax.div(q, TILE) * SLOTS, lax.rem(q, TILE)
            grp, qrow = lax.div(q, ROWS) - COLS_AXIS - col, lax.rem(q, ROWS)
            is_own = grp == 0
            is_near = jnp.logical_or(is_own, grp == 1 - 2 * core)
            base = qrow * QUARTER
            at = [jnp.int32(-1)] * QUARTER
            for u in range(SLOTS):
                v = pat[side + u, lane]
                for s in range(QUARTER):
                    at[s] = jnp.where(v == wanted[s], base + (u // 2) * BLOCKS + u % 2, at[s])
            for s in range(QUARTER):
                hit = jnp.logical_and(at[s] >= 0, is_near)
                tab_near[r * 16 + t * 2 + s] = jnp.where(
                    hit, at[s] + jnp.where(is_own, 0, GROUP), 2 * GROUP
                )
            is_far = jnp.logical_not(is_near)
            for j in range(min(t + 1, REACH)):
                here_j = jnp.logical_and(is_far, count == j)
                far_t[j] = jnp.where(here_j, t, far_t[j])
                for s in range(QUARTER):
                    far_at[j][s] = jnp.where(jnp.logical_and(here_j, at[s] >= 0), at[s], far_at[j][s])
            count = count + is_far.astype(jnp.int32)
        for j in range(SLOTS):
            tab_t[r * SLOTS + j] = far_t[j]
            for s in range(QUARTER):
                tab_part[r * 16 + j * 2 + s] = far_at[j][s]
        return carry

    lax.fori_loop(0, ROWS, index_row, 0)

    for j in range(CHUNKS):
        k = later(j)
        arrived(own(dn, j), own_sem(dn, j))
        arrived(own(up, k), own_sem(up, k))
        send(own(dn, j), halo(dn, j), halo_sem(dn, j), at_part, close)
        send(own(up, k), halo(up, k), halo_sem(up, k), at_part, close)
        if j < half:
            send(own(dn, j), own(dn, j), own_sem(dn, j), at_up)
            send(own(up, k), own(up, k), own_sem(up, k), at_dn)
        send(own(dn, j), mate(dn, j), mate_sem(dn, j), at_mate)
        send(own(up, k), mate(up, k), mate_sem(up, k), at_mate)
    for j in range(CHUNKS):
        arrived(halo(l, j), halo_sem(l, j))
        send(halo(l, j), halo(l, j), halo_sem(l, j), at_up, far)
        send(halo(l, j), halo(l, j), halo_sem(l, j), at_dn, far)
    for j in range(half):
        for k in (j, j + half):
            arrived(own(opp, k), own_sem(opp, k))
            send(own(opp, k), mate(opp, k), mate_sem(opp, k), at_mate)
            if k in DIRECT:
                send(own(opp, k), halo(opp, k), halo_sem(opp, k), at_part, give)
    for j in range(half):
        arrived(halo(dn, j), halo_sem(dn, j))
        send(halo(dn, j), halo(dn, j), halo_sem(dn, j), at_up, keep if j in DIRECT else None)
        arrived(halo(up, j + half), halo_sem(up, j + half))
        send(halo(up, j + half), halo(up, j + half), halo_sem(up, j + half), at_dn, keep if j + half in DIRECT else None)
    for j in range(half):
        arrived(halo(dn, j + half), halo_sem(dn, j + half))
        arrived(halo(up, j), halo_sem(up, j))
    mine.wait()
    for layer in range(LAYERS):
        for j in range(CHUNKS):
            arrived(mate(layer, j), mate_sem(layer, j))

    def split(v):
        hi = v.astype(jnp.bfloat16)
        return hi, (v - hi.astype(jnp.float32)).astype(jnp.bfloat16)

    def product(r, ref, tab):
        for t in range(SLOTS):
            for s in range(QUARTER):
                hi, lo = split(ref[tab[r * 16 + t * 2 + s]])
                m_hi[t * BS:(t + 1) * BS, s * BS:(s + 1) * BS] = hi
                m_lo[t * BS:(t + 1) * BS, s * BS:(s + 1) * BS] = lo
        h, low = (jnp.concatenate([a[r * SLOTS + t] for t in range(SLOTS)], axis=1) for a in (a_hi, a_lo))
        w = m_hi[...]
        total = jnp.dot(h, w, preferred_element_type=jnp.float32)
        total += jnp.dot(h, m_lo[...], preferred_element_type=jnp.float32)
        return total + jnp.dot(low, w, preferred_element_type=jnp.float32)

    def near_row(r, carry):
        for t in range(SLOTS):
            hi, lo = split(near[(t // 2) * BLOCKS + r * QUARTER + t % 2])
            a_hi[r * SLOTS + t] = hi
            a_lo[r * SLOTS + t] = lo
        total = product(r, near, tab_near)
        for s in range(QUARTER):
            acc[r * QUARTER + s] = total[:, s * BS:(s + 1) * BS]
        return carry

    lax.fori_loop(0, ROWS, near_row, 0)

    for j in range(CHUNKS):
        arrived(halo(opp, j), halo_sem(opp, j))

    def pair(r, j):
        tiles = [[split(part[tab_part[r * 16 + i * 2 + s]]) for s in range(QUARTER)] for i in (j, j + 1)]
        w_hi, w_lo = (
            jnp.concatenate([jnp.concatenate([b[k] for b in tile], axis=1) for tile in tiles], axis=0) for k in (0, 1)
        )
        h, low = (jnp.concatenate([a[r * SLOTS + tab_t[r * SLOTS + i]] for i in (j, j + 1)], axis=1) for a in (a_hi, a_lo))
        total = jnp.dot(h, w_hi, preferred_element_type=jnp.float32)
        total += jnp.dot(h, w_lo, preferred_element_type=jnp.float32)
        return total + jnp.dot(low, w_hi, preferred_element_type=jnp.float32)

    for i in range(ROWS):
        r = i + core * (ROWS - 1 - 2 * i)
        total = pair(r, 0)
        for j in range(2, min(REACH, ROWS - i), 2):
            total += pair(r, j)
        for s in range(QUARTER):
            out_ref[r * QUARTER + s] = acc[r * QUARTER + s] + total[:, s * BS:(s + 1) * BS]
    for copy, when in sent:
        if when is None:
            copy.wait_send()
        else:
            pl.when(when)(copy.wait_send)


def per_device(pattern, density):
    shape = density.shape
    flat = density.reshape(BLOCKS, BS, BS)
    f32, bf16 = jnp.float32, jnp.bfloat16
    result = pl.pallas_call(
        kernel,
        out_shape=jax.ShapeDtypeStruct((BLOCKS, BS, BS), f32),
        in_specs=[pl.BlockSpec(memory_space=pl.ANY)] * 2,
        out_specs=pl.BlockSpec(memory_space=pltpu.VMEM),
        scratch_shapes=[
            pltpu.VMEM((2 * GROUP + 1, BS, BS), f32),
            pltpu.VMEM((GROUP + 1, BS, BS), f32),
            pltpu.SMEM((3 * SLOTS, TILE), jnp.int32),
            pltpu.SMEM((ROWS * SLOTS * QUARTER,), jnp.int32),
            pltpu.SMEM((ROWS * SLOTS * QUARTER,), jnp.int32),
            pltpu.SMEM((ROWS * SLOTS,), jnp.int32),
            pltpu.VMEM((ROWS * SLOTS, BS, BS), bf16),
            pltpu.VMEM((ROWS * SLOTS, BS, BS), bf16),
            pltpu.VMEM((SLOTS * BS, QUARTER * BS), bf16),
            pltpu.VMEM((SLOTS * BS, QUARTER * BS), bf16),
            pltpu.VMEM((BLOCKS, BS, BS), f32),
            pltpu.SemaphoreType.DMA((2 * LAYERS * CHUNKS,)),
            pltpu.SemaphoreType.DMA((LAYERS * CHUNKS,)),
            pltpu.SemaphoreType.DMA((13 * CHUNKS + len(DIRECT),)),
            pltpu.SemaphoreType.DMA,
            pltpu.SemaphoreType.DMA((3,)),
        ],
        compiler_params=pltpu.CompilerParams(
            collective_id=0, has_side_effects=True, vmem_limit_bytes=52 * 1024 * 1024
        ),
        cost_estimate=pl.CostEstimate(flops=3 * 2**29, bytes_accessed=2**24, transcendentals=0),
    )(pattern.T, flat)
    return result.reshape(shape)


def solution(mesh):
    in_specs = (P(), P(("row", "col"), "layer", None, None))
    out_specs = P(("row", "col"), "layer", None, None)
    return jax.shard_map(
        per_device, mesh=mesh, in_specs=in_specs, out_specs=out_specs, check_vma=False
    )
```

```python
import jax
import jax.numpy as jnp
from jax import lax
from jax.experimental import pallas as pl
from jax.experimental.pallas import tpu as pltpu
from jax.sharding import PartitionSpec as P

MESH = pl.DeviceIdType.MESH
LAYERS, ROWS_AXIS, COLS_AXIS, RUNS = 4, 8, 16, 4
ROWS, SLOTS, QUARTER, BS = 8, 8, 2, 128
BLOCKS = ROWS * QUARTER
GROUP = LAYERS * BLOCKS
TILE = COLS_AXIS * ROWS
REACH = SLOTS - 1
CHUNKS = 4
AHEAD = 4
DIRECT = (0, 2, 3)
CB = BLOCKS // CHUNKS


def kernel(
    pat_ref, den_ref, out_ref,
    near, part, pat, tab_near, tab_part, tab_t, a_hi, a_lo, m_hi, m_lo, acc,
    near_sem, part_sem, send_sem, local_sem, pat_sem,
):
    l, row, col = (lax.axis_index(a) for a in ("layer", "row", "col"))
    core = lax.rem(col, 2)
    g = row * COLS_AXIS + col
    up, dn, opp = lax.rem(l + 1, 4), lax.rem(l + 3, 4), lax.rem(l + 2, 4)
    pg = lax.rem(g + jnp.where(core == 0, 127, 1), 128)
    at_up, at_dn = (up, row, col), (dn, row, col)
    at_mate = (l, row, col + 1 - 2 * core)
    at_part = (l, lax.div(pg, COLS_AXIS), lax.rem(pg, COLS_AXIS))

    def long_way(at_row, at_col):
        at_x = lax.rem(at_row, RUNS)
        return jnp.logical_or(
            jnp.logical_and(at_col == 0, at_x != 0),
            jnp.logical_and(at_col == COLS_AXIS - 1, at_x != RUNS - 1),
        )

    def mate_col(at_col):
        return at_col + 1 - 2 * lax.rem(at_col, 2)

    far = long_way(row, col)
    close = jnp.logical_not(far)
    keep = jnp.logical_not(long_way(row, mate_col(col)))
    give = long_way(at_part[1], mate_col(at_part[2]))

    barrier = pltpu.get_barrier_semaphore()
    for peer in (at_up, at_dn, at_mate, at_part):
        pl.semaphore_signal(barrier, inc=1, device_id=peer, device_id_type=MESH)

    sent = []

    def send(src, dst, sem, peer, when=None):
        n = len(sent)
        copy = pltpu.make_async_remote_copy(
            src_ref=src, dst_ref=dst, send_sem=send_sem.at[n], recv_sem=sem,
            device_id=peer, device_id_type=MESH,
        )
        sent.append((copy, when))
        if when is None:
            copy.start()
        else:
            pl.when(when)(copy.start)

    def piece(ref, base, layer, j):
        return ref.at[pl.ds(base + layer * BLOCKS + j * CB, CB)]

    def own(layer, j):
        return piece(near, 0, layer, j)

    def mate(layer, j):
        return piece(near, GROUP, layer, j)

    def halo(layer, j):
        return piece(part, 0, layer, j)

    def own_sem(layer, j):
        return near_sem.at[layer * CHUNKS + j]

    def mate_sem(layer, j):
        return near_sem.at[LAYERS * CHUNKS + layer * CHUNKS + j]

    def halo_sem(layer, j):
        return part_sem.at[layer * CHUNKS + j]

    def arrived(ref, sem):
        pltpu.make_async_remote_copy(
            src_ref=ref, dst_ref=ref, send_sem=send_sem.at[0], recv_sem=sem,
            device_id=at_mate, device_id_type=MESH,
        ).wait_recv()

    pat_copies = []
    for k in range(3):
        tile = lax.rem(row + ROWS_AXIS - 1 + k, ROWS_AXIS)
        c = pltpu.make_async_copy(
            pat_ref.at[:, pl.ds(pl.multiple_of(tile * TILE, TILE), TILE)], pat.at[pl.ds(k * SLOTS, SLOTS)], pat_sem.at[k]
        )
        c.start()
        pat_copies.append(c)
    mine = pltpu.make_async_copy(den_ref, near.at[pl.ds(l * BLOCKS, BLOCKS)], local_sem)
    mine.start()
    pl.semaphore_wait(barrier, 4)

    def spread(j):
        src = den_ref.at[pl.ds(j * CB, CB)]
        send(src, own(l, j), own_sem(l, j), at_up)
        send(src, own(l, j), own_sem(l, j), at_dn)

    for j in range(CHUNKS):
        src = den_ref.at[pl.ds(j * CB, CB)]
        if j < AHEAD:
            spread(j)
        send(src, halo(l, j), halo_sem(l, j), at_part)
    for j in range(CHUNKS):
        src = den_ref.at[pl.ds(j * CB, CB)]
        send(src, mate(l, j), mate_sem(l, j), at_mate)

    near[2 * GROUP] = jnp.zeros((BS, BS), jnp.float32)
    part[GROUP] = jnp.zeros((BS, BS), jnp.float32)
    for c in pat_copies:
        c.wait()

    def index_row(r, carry):
        here = col * ROWS + r
        wanted = [pat[SLOTS + 2 * l + s, here] for s in range(QUARTER)]
        count = jnp.int32(0)
        far_t = [jnp.int32(0)] * SLOTS
        far_at = [[jnp.int32(GROUP)] * QUARTER for _ in range(SLOTS)]
        for t in range(SLOTS):
            q = jnp.clip(pat[SLOTS + t, here] - TILE * (row - 1), 0, 3 * TILE - 1)
            side, lane = lax.div(q, TILE) * SLOTS, lax.rem(q, TILE)
            grp, qrow = lax.div(q, ROWS) - COLS_AXIS - col, lax.rem(q, ROWS)
            is_own = grp == 0
            is_near = jnp.logical_or(is_own, grp == 1 - 2 * core)
            base = qrow * QUARTER
            at = [jnp.int32(-1)] * QUARTER
            for u in range(SLOTS):
                v = pat[side + u, lane]
                for s in range(QUARTER):
                    at[s] = jnp.where(v == wanted[s], base + (u // 2) * BLOCKS + u % 2, at[s])
            for s in range(QUARTER):
                hit = jnp.logical_and(at[s] >= 0, is_near)
                tab_near[r * 16 + t * 2 + s] = jnp.where(
                    hit, at[s] + jnp.where(is_own, 0, GROUP), 2 * GROUP
                )
            is_far = jnp.logical_not(is_near)
            for j in range(min(t + 1, REACH)):
                here_j = jnp.logical_and(is_far, count == j)
                far_t[j] = jnp.where(here_j, t, far_t[j])
                for s in range(QUARTER):
                    far_at[j][s] = jnp.where(jnp.logical_and(here_j, at[s] >= 0), at[s], far_at[j][s])
            count = count + is_far.astype(jnp.int32)
        for j in range(SLOTS):
            tab_t[r * SLOTS + j] = far_t[j]
            for s in range(QUARTER):
                tab_part[r * 16 + j * 2 + s] = far_at[j][s]
        return carry

    lax.fori_loop(0, ROWS, index_row, 0)

    half = CHUNKS // 2
    for j in range(CHUNKS):
        arrived(own(dn, j), own_sem(dn, j))
        arrived(own(up, j), own_sem(up, j))
        if j + AHEAD < CHUNKS:
            spread(j + AHEAD)
        if j < half:
            send(own(dn, j), own(dn, j), own_sem(dn, j), at_up)
        else:
            send(own(up, j), own(up, j), own_sem(up, j), at_dn)
        if j < half:
            send(own(dn, j), halo(dn, j), halo_sem(dn, j), at_part, close)
        else:
            send(own(up, j), halo(up, j), halo_sem(up, j), at_part, close)
        send(own(dn, j), mate(dn, j), mate_sem(dn, j), at_mate)
        send(own(up, j), mate(up, j), mate_sem(up, j), at_mate)
    for j in range(half):
        send(own(dn, j + half), halo(dn, j + half), halo_sem(dn, j + half), at_part, close)
        send(own(up, j), halo(up, j), halo_sem(up, j), at_part, close)
    for j in range(CHUNKS):
        arrived(halo(l, j), halo_sem(l, j))
        send(halo(l, j), halo(l, j), halo_sem(l, j), at_up, far)
        send(halo(l, j), halo(l, j), halo_sem(l, j), at_dn, far)
    for j in range(half):
        for k in (j, j + half):
            arrived(own(opp, k), own_sem(opp, k))
            send(own(opp, k), mate(opp, k), mate_sem(opp, k), at_mate)
            if k in DIRECT:
                send(own(opp, k), halo(opp, k), halo_sem(opp, k), at_part, give)
    for j in range(half):
        arrived(halo(dn, j), halo_sem(dn, j))
        send(halo(dn, j), halo(dn, j), halo_sem(dn, j), at_up, keep if j in DIRECT else None)
        arrived(halo(up, j + half), halo_sem(up, j + half))
        send(halo(up, j + half), halo(up, j + half), halo_sem(up, j + half), at_dn, keep if j + half in DIRECT else None)
    for j in range(half):
        arrived(halo(dn, j + half), halo_sem(dn, j + half))
        arrived(halo(up, j), halo_sem(up, j))
    mine.wait()
    for layer in range(LAYERS):
        for j in range(CHUNKS):
            arrived(mate(layer, j), mate_sem(layer, j))

    def split(v):
        hi = v.astype(jnp.bfloat16)
        return hi, (v - hi.astype(jnp.float32)).astype(jnp.bfloat16)

    def product(r, ref, tab):
        for t in range(SLOTS):
            for s in range(QUARTER):
                hi, lo = split(ref[tab[r * 16 + t * 2 + s]])
                m_hi[t * BS:(t + 1) * BS, s * BS:(s + 1) * BS] = hi
                m_lo[t * BS:(t + 1) * BS, s * BS:(s + 1) * BS] = lo
        h, low = (jnp.concatenate([a[r * SLOTS + t] for t in range(SLOTS)], axis=1) for a in (a_hi, a_lo))
        w = m_hi[...]
        total = jnp.dot(h, w, preferred_element_type=jnp.float32)
        total += jnp.dot(h, m_lo[...], preferred_element_type=jnp.float32)
        return total + jnp.dot(low, w, preferred_element_type=jnp.float32)

    def near_row(r, carry):
        for t in range(SLOTS):
            hi, lo = split(near[(t // 2) * BLOCKS + r * QUARTER + t % 2])
            a_hi[r * SLOTS + t] = hi
            a_lo[r * SLOTS + t] = lo
        total = product(r, near, tab_near)
        for s in range(QUARTER):
            acc[r * QUARTER + s] = total[:, s * BS:(s + 1) * BS]
        return carry

    lax.fori_loop(0, ROWS, near_row, 0)

    for j in range(CHUNKS):
        arrived(halo(opp, j), halo_sem(opp, j))

    def pair(r, j):
        tiles = [[split(part[tab_part[r * 16 + i * 2 + s]]) for s in range(QUARTER)] for i in (j, j + 1)]
        w_hi, w_lo = (
            jnp.concatenate([jnp.concatenate([b[k] for b in tile], axis=1) for tile in tiles], axis=0) for k in (0, 1)
        )
        h, low = (jnp.concatenate([a[r * SLOTS + tab_t[r * SLOTS + i]] for i in (j, j + 1)], axis=1) for a in (a_hi, a_lo))
        total = jnp.dot(h, w_hi, preferred_element_type=jnp.float32)
        total += jnp.dot(h, w_lo, preferred_element_type=jnp.float32)
        return total + jnp.dot(low, w_hi, preferred_element_type=jnp.float32)

    for i in range(ROWS):
        r = i + core * (ROWS - 1 - 2 * i)
        total = pair(r, 0)
        for j in range(2, min(REACH, ROWS - i), 2):
            total += pair(r, j)
        for s in range(QUARTER):
            out_ref[r * QUARTER + s] = acc[r * QUARTER + s] + total[:, s * BS:(s + 1) * BS]
    for copy, when in sent:
        if when is None:
            copy.wait_send()
        else:
            pl.when(when)(copy.wait_send)


def per_device(pattern, density):
    shape = density.shape
    flat = density.reshape(BLOCKS, BS, BS)
    f32, bf16 = jnp.float32, jnp.bfloat16
    result = pl.pallas_call(
        kernel,
        out_shape=jax.ShapeDtypeStruct((BLOCKS, BS, BS), f32),
        in_specs=[pl.BlockSpec(memory_space=pl.ANY)] * 2,
        out_specs=pl.BlockSpec(memory_space=pltpu.VMEM),
        scratch_shapes=[
            pltpu.VMEM((2 * GROUP + 1, BS, BS), f32),
            pltpu.VMEM((GROUP + 1, BS, BS), f32),
            pltpu.SMEM((3 * SLOTS, TILE), jnp.int32),
            pltpu.SMEM((ROWS * SLOTS * QUARTER,), jnp.int32),
            pltpu.SMEM((ROWS * SLOTS * QUARTER,), jnp.int32),
            pltpu.SMEM((ROWS * SLOTS,), jnp.int32),
            pltpu.VMEM((ROWS * SLOTS, BS, BS), bf16),
            pltpu.VMEM((ROWS * SLOTS, BS, BS), bf16),
            pltpu.VMEM((SLOTS * BS, QUARTER * BS), bf16),
            pltpu.VMEM((SLOTS * BS, QUARTER * BS), bf16),
            pltpu.VMEM((BLOCKS, BS, BS), f32),
            pltpu.SemaphoreType.DMA((2 * LAYERS * CHUNKS,)),
            pltpu.SemaphoreType.DMA((LAYERS * CHUNKS,)),
            pltpu.SemaphoreType.DMA((13 * CHUNKS + len(DIRECT),)),
            pltpu.SemaphoreType.DMA,
            pltpu.SemaphoreType.DMA((3,)),
        ],
        compiler_params=pltpu.CompilerParams(
            collective_id=0, has_side_effects=True, vmem_limit_bytes=52 * 1024 * 1024
        ),
        cost_estimate=pl.CostEstimate(flops=3 * 2**29, bytes_accessed=2**24, transcendentals=0),
    )(pattern.T, flat)
    return result.reshape(shape)


def solution(mesh):
    in_specs = (P(), P(("row", "col"), "layer", None, None))
    out_specs = P(("row", "col"), "layer", None, None)
    return jax.shard_map(
        per_device, mesh=mesh, in_specs=in_specs, out_specs=out_specs, check_vma=False
    )
```
